32 devices in a mesh: space: 4 (over z), section: 4 (over y, x), rep: 2 (over core).
Axes of the slice: x: 2, y: 2, z: 4, core: 2. Of those that a mesh axis runs over, the one named last changes fastest.
Arguments:
- feats: bfloat16 [4, 16, 40, 256], P('rep', 'space'), may hold values from -6 to 6
- labels: int32 [4, 16, 40], P('rep', 'space'), may hold values from 0 to 2
- class_weight: int32 [3], replicated, may hold values from 1 to 9
- depth_kernel: bfloat16 [4, 3, 9, 256], P('section'), may hold values from -2 to 2
- point_weight: bfloat16 [4, 4, 256, 256], P('section'), may hold values from -0.375 to 0.375
- proj_weight: bfloat16 [4, 1024, 256], P('section'), may hold values from -0.1875 to 0.1875
- head_weight: bfloat16 [4, 256, 3], P('section'), may hold values from -0.375 to 0.375
Outputs:
- kernel_grad: float32 [4, 3, 9, 256], P('section')
- point_grad: float32 [4, 4, 256, 256], P('section')
- proj_grad: float32 [4, 1024, 256], P('section')
- head_grad: float32 [4, 256, 3], P('section')
The draws below stay inside these ranges and needn't reach their ends.
All inputs are finite; a program needn't handle non-finite values.
Results may differ from the reference program's by a relative error of at most 0.013.
The reference program's roundings to bfloat16 on the way count: a program that leaves them out, or rounds other values in their place, can miss the bound.
Values may be sent and summed in bfloat16 or wider, within the bound.
A program may use at most 128 MiB of HBM per device.

```python
import jax
import jax.numpy as jnp
from jax import lax

C = 256
COLS = 40
SECTIONS = 4
H = 16
SNAPS = 4


def with_ends(values, key, smallest, top_value):
    longest = values.shape.index(max(values.shape))
    spots = []
    for shift in (0, 1):
        where = [jax.random.randint(jax.random.fold_in(key, axis), (), 0, length) for axis, length in enumerate(values.shape)]
        where[longest] = (where[longest] + shift) % values.shape[longest]
        spots.append(tuple(where))
    return values.at[spots[0]].set(smallest).at[spots[1]].set(top_value)


def levels(rng, extent, split, low, top_value):
    loudness = 1.0
    for position, blocks in split:
        heights = jax.random.uniform(jax.random.fold_in(jax.random.fold_in(rng, 6), position), (blocks,), jnp.float32, low / len(split), top_value / len(split))
        loudness = loudness * jnp.repeat(jnp.exp(heights), extent[position] // blocks).reshape((-1,) + (1,) * (len(extent) - 1 - position))
    return loudness


def noise(rng, shape, width, bound, cuts=(), kind=jnp.bfloat16):
    gain = levels(rng, shape, cuts, -0.22, 0.18) if cuts else 1.0
    values = jax.random.normal(rng, shape, jnp.float32) * width * gain
    return jnp.minimum(jnp.maximum(values, -bound), bound).astype(kind)


def setup_inputs(seed: int = 0) -> dict:
    key_of = jax.random.split(jax.random.key(seed), 8)
    feats = noise(key_of[0], (SNAPS, H, COLS, C), 1.0, 6.0, ((0, 2), (1, 4)))
    labels = with_ends(jax.random.randint(key_of[1], (SNAPS, H, COLS), 0, 3), jax.random.fold_in(key_of[1], 1), 0, 2).astype(jnp.int32)
    class_weight = jax.random.randint(key_of[2], (3,), 1, 10).astype(jnp.int32)
    depth_kernel = noise(key_of[3], (SECTIONS, 3, 9, C), 9 ** -0.5, 2.0, ((0, 4),))
    point_weight = noise(key_of[4], (SECTIONS, 4, C, C), C ** -0.5, 0.375, ((0, 4),))
    proj_weight = noise(key_of[5], (SECTIONS, 4 * C, C), (4 * C) ** -0.5, 0.1875, ((0, 4),))
    head_weight = noise(key_of[6], (SECTIONS, C, 3), C ** -0.5, 0.375, ((0, 4),))
    return dict(feats=feats, labels=labels, class_weight=class_weight, depth_kernel=depth_kernel, point_weight=point_weight, proj_weight=proj_weight, head_weight=head_weight)


spacings = (12, 24, 36)
loss_scale = 256.0


def moved(source, offset, axis_dim):
    length = source.shape[axis_dim]
    if abs(offset) >= length:
        return jnp.zeros_like(source)
    widths = [(0, 0)] * source.ndim
    widths[axis_dim] = (max(-offset, 0), max(offset, 0))
    padded = jnp.pad(source, widths)
    begin_at = max(offset, 0)
    return lax.slice_in_dim(padded, begin_at, begin_at + length, axis=axis_dim)


def depthwise(source, tap_weights, spacing):
    running = jnp.zeros(source.shape, jnp.float32)
    for row_tap in (-1, 0, 1):
        row_moved = moved(source, row_tap * spacing, 0)
        for col_tap in (-1, 0, 1):
            running = running + tap_weights[3 * (row_tap + 1) + col_tap + 1] * moved(row_moved, col_tap * spacing, 1)
    return running


def depthwise_back(grads, base_map, tap_weights, spacing):
    running = jnp.zeros(grads.shape, jnp.float32)
    kernel_rows = []
    for row_tap in (-1, 0, 1):
        row_moved = moved(grads, -row_tap * spacing, 0)
        for col_tap in (-1, 0, 1):
            shifted = moved(row_moved, -col_tap * spacing, 1)
            running = running + tap_weights[3 * (row_tap + 1) + col_tap + 1] * shifted
            kernel_rows.append(jnp.sum(shifted * base_map, axis=(0, 1)))
    return running, jnp.stack(kernel_rows)


def matmul(first_op, second_op):
    return jnp.dot(first_op, second_op, preferred_element_type=jnp.float32)


def outer(first_op, second_op):
    return lax.dot_general(first_op, second_op, (((0,), (0,)), ((), ())), preferred_element_type=jnp.float32)


def reference(feats, labels, class_weight, depth_kernel, point_weight, proj_weight, head_weight):
    pixels = H * COLS
    factor = loss_scale / (SNAPS * H * COLS)
    weight_table = class_weight.astype(jnp.float32)
    class_ids = jnp.arange(3, dtype=jnp.int32)
    kernel_acc = [jnp.zeros((3, 9, C), jnp.float32) for section_no in range(SECTIONS)]
    point_acc = [jnp.zeros((4, C, C), jnp.float32) for section_no in range(SECTIONS)]
    proj_acc = [jnp.zeros((4 * C, C), jnp.float32) for section_no in range(SECTIONS)]
    head_acc = [jnp.zeros((C, 3), jnp.float32) for section_no in range(SECTIONS)]
    for sample in range(SNAPS):
        label_flat = labels[sample].reshape(pixels, 1)
        onehot = (label_flat == class_ids[None, :]).astype(jnp.float32)
        pixel_weight = jnp.sum(onehot * weight_table[None, :], axis=1)
        current = feats[sample]
        records = []
        for section_no in range(SECTIONS):
            tap_weights = depth_kernel[section_no].astype(jnp.float32)
            plain_in = current.astype(jnp.float32)
            flat_in = current.reshape(pixels, C)
            branch_maps = [depthwise(plain_in, tap_weights[branch], spacings[branch]).astype(jnp.bfloat16) for branch in range(3)]
            pre_acts = [matmul(branch_maps[branch].reshape(pixels, C), point_weight[section_no, branch]) for branch in range(3)]
            pre_acts.append(matmul(flat_in, point_weight[section_no, 3]))
            joined = jnp.concatenate([jnp.maximum(pre_act, 0.0).astype(jnp.bfloat16) for pre_act in pre_acts], axis=1)
            mixed_pre = matmul(joined, proj_weight[section_no])
            result = (flat_in.astype(jnp.float32) + jnp.maximum(mixed_pre, 0.0)).astype(jnp.bfloat16)
            logits = matmul(result, head_weight[section_no])
            chances = jax.nn.softmax(logits, axis=1)
            head_delta = ((factor * pixel_weight)[:, None] * (chances - onehot)).astype(jnp.bfloat16)
            head_acc[section_no] = head_acc[section_no] + outer(result, head_delta)
            from_head = matmul(head_delta, head_weight[section_no].T)
            records.append((tap_weights, plain_in, flat_in, branch_maps, joined, mixed_pre, from_head))
            current = result.reshape(H, COLS, C)
        incoming = jnp.zeros((pixels, C), jnp.float32)
        for section_no in reversed(range(SECTIONS)):
            tap_weights, plain_in, flat_in, branch_maps, joined, mixed_pre, from_head = records[section_no]
            total_grad = from_head + incoming
            gate_mixed = jnp.where(mixed_pre > 0, total_grad, 0.0).astype(jnp.bfloat16)
            proj_acc[section_no] = proj_acc[section_no] + outer(joined, gate_mixed)
            back_joined = matmul(gate_mixed, proj_weight[section_no].T)
            gate_joined = jnp.where(joined > 0, back_joined, 0.0).astype(jnp.bfloat16)
            spread = jnp.zeros((H, COLS, C), jnp.float32)
            point_terms = []
            kernel_terms = []
            for branch in range(3):
                part_grad = gate_joined[:, branch * C:(branch + 1) * C]
                point_terms.append(outer(branch_maps[branch].reshape(pixels, C), part_grad))
                branch_grad = matmul(part_grad, point_weight[section_no, branch].T).astype(jnp.bfloat16)
                back_map, tap_grad = depthwise_back(branch_grad.reshape(H, COLS, C).astype(jnp.float32), plain_in, tap_weights[branch], spacings[branch])
                spread = spread + back_map
                kernel_terms.append(tap_grad)
            part_grad = gate_joined[:, 3 * C:]
            point_terms.append(outer(flat_in, part_grad))
            plain_back = matmul(part_grad, point_weight[section_no, 3].T)
            point_acc[section_no] = point_acc[section_no] + jnp.stack(point_terms)
            kernel_acc[section_no] = kernel_acc[section_no] + jnp.stack(kernel_terms)
            input_grad = (total_grad + plain_back + spread.reshape(pixels, C)).astype(jnp.bfloat16)
            incoming = lax.optimization_barrier(input_grad).astype(jnp.float32)
    return (jnp.stack(kernel_acc), jnp.stack(point_acc), jnp.stack(proj_acc), jnp.stack(head_acc))
```

```python
import functools

import jax
import jax.numpy as jnp
from jax import lax
from jax.experimental import pallas as pl
from jax.experimental.pallas import tpu as pltpu
from jax.sharding import PartitionSpec as P

spacings = (12, 24, 36)
loss_scale = 256.0


def passed_along(block, axis, distance):
    devices = range(lax.axis_size(axis))
    route = [(i - distance, i) for i in devices if i - distance in devices]
    return lax.ppermute(block, axis, route)


def moved(source, offset, axis_dim):
    length = source.shape[axis_dim]
    widths = [(0, 0)] * source.ndim
    widths[axis_dim] = (max(-offset, 0), max(offset, 0))
    padded = jnp.pad(source, widths)
    begin_at = max(offset, 0)
    return lax.slice_in_dim(padded, begin_at, begin_at + length, axis=axis_dim)


def make_view(shift_rows, device_count):

    def piece_from(source, devices_ahead):
        if devices_ahead >= device_count or -devices_ahead >= device_count:
            return jnp.zeros_like(source)
        return shift_rows(source, -devices_ahead)

    def view(source, offset):
        if offset == 0:
            return source
        tile_rows = source.shape[0]
        whole_part = offset // tile_rows
        return piece_from(source, whole_part)

    return view


def forward_taps(row_views, tap_weights, col_step):
    running = jnp.zeros(row_views[0].shape, jnp.float32)
    for row_tap in (-1, 0, 1):
        for col_tap in (-1, 0, 1):
            running = running + tap_weights[3 * (row_tap + 1) + col_tap + 1] * moved(
                row_views[row_tap], col_tap * col_step, 1
            )
    return running


def backward_taps(row_views, base_map, tap_weights, col_step):
    base_wide = base_map.astype(jnp.float32)
    running = jnp.zeros(base_map.shape, jnp.float32)
    kernel_rows = []
    for row_tap in (-1, 0, 1):
        for col_tap in (-1, 0, 1):
            shifted = moved(row_views[row_tap], -col_tap * col_step, 1)
            running = running + tap_weights[3 * (row_tap + 1) + col_tap + 1] * shifted
            partial_sum = jnp.sum(shifted * base_wide, axis=0)
            kernel_rows.append(jnp.sum(partial_sum, axis=0))
    return (running, jnp.stack(kernel_rows))


def matmul(first_op, second_op):
    return jnp.dot(first_op, second_op, preferred_element_type=jnp.float32)


def matmul_trans(first_op, second_op):
    return lax.dot_general(
        first_op, second_op, (((1,), (1,)), ((), ())), preferred_element_type=jnp.float32
    )


def outer(first_op, second_op):
    return lax.dot_general(
        first_op, second_op, (((0,), (0,)), ((), ())), preferred_element_type=jnp.float32
    )


def store(buffer, batch_slot, is_valid, new_value):
    old_value = lax.dynamic_index_in_dim(buffer, batch_slot, 0, keepdims=False)
    return lax.dynamic_update_index_in_dim(
        buffer, jnp.where(is_valid, new_value, old_value), batch_slot, 0
    )


def fetch(buffer, batch_slot):
    return lax.dynamic_index_in_dim(buffer, batch_slot, 0, keepdims=False)


def forward_block(current, weights, label_tile, tools, factor, weight_table):
    taps_all, flat_taps, point_mats, proj_mat, head_mat = weights
    view_fn, to_maps, from_maps = (tools[0], tools[1], tools[2])
    tile_rows, width_cols, channels = current.shape
    pixels = tile_rows * width_cols
    branch_list = []
    for branch, spacing in enumerate(spacings):
        row_views = {
            row_tap: view_fn(current, row_tap * spacing).astype(jnp.float32)
            for row_tap in (-1, 0, 1)
        }
        branch_list.append(forward_taps(row_views, taps_all[branch], spacing).astype(jnp.bfloat16))
    branch_out = jnp.stack(branch_list).reshape(3, pixels, channels)
    extra = ()
    flat_in = current.reshape(pixels, channels)
    pre_acts = [matmul(branch_out[branch], point_mats[branch]) for branch in range(3)]
    pre_acts.append(matmul(flat_in, point_mats[3]))
    joined = jnp.concatenate(
        [jnp.maximum(pre_act, 0.0).astype(jnp.bfloat16) for pre_act in pre_acts], axis=1
    )
    mixed_pre = matmul(joined, proj_mat)
    result = (flat_in.astype(jnp.float32) + jnp.maximum(mixed_pre, 0.0)).astype(jnp.bfloat16)
    logits = matmul(result, head_mat)
    class_ids = jnp.arange(3, dtype=jnp.int32)
    label_flat = label_tile.reshape(pixels, 1)
    onehot = (label_flat == class_ids[None, :]).astype(jnp.float32)
    pixel_weight = jnp.sum(onehot * weight_table[None, :], axis=1)
    chances = jax.nn.softmax(logits, axis=1)
    head_delta = ((factor * pixel_weight)[:, None] * (chances - onehot)).astype(jnp.bfloat16)
    head_term = outer(result, head_delta)
    from_head = matmul_trans(head_delta, head_mat)
    record = (current, branch_out, joined, mixed_pre, from_head) + extra
    return (result.reshape(tile_rows, width_cols, channels), head_term, record)


def backward_block(record, incoming, weights, tools):
    taps_all, flat_taps, point_mats, proj_mat, head_mat = weights
    view_fn, grads_to, grads_from = (tools[0], tools[3], tools[4])
    current, branch_out, joined, mixed_pre, from_head = (
        record[0],
        record[1],
        record[2],
        record[3],
        record[4],
    )
    tile_rows, width_cols, channels = current.shape
    pixels = tile_rows * width_cols
    total_grad = from_head + incoming
    gate_mixed = jnp.where(mixed_pre > 0, total_grad, 0.0).astype(jnp.bfloat16)
    proj_term = outer(joined, gate_mixed)
    back_joined = matmul_trans(gate_mixed, proj_mat)
    gate_joined = jnp.where(joined > 0, back_joined, 0.0).astype(jnp.bfloat16)
    flat_in = current.reshape(pixels, channels)
    point_terms = []
    branch_grads = []
    for branch in range(3):
        part_grad = gate_joined[:, branch * channels : (branch + 1) * channels]
        point_terms.append(outer(branch_out[branch], part_grad))
        branch_grads.append(matmul_trans(part_grad, point_mats[branch]).astype(jnp.bfloat16))
    part_grad = gate_joined[:, 3 * channels :]
    point_terms.append(outer(flat_in, part_grad))
    plain_back = matmul_trans(part_grad, point_mats[3])
    grads_stack = jnp.stack(branch_grads).reshape(3, tile_rows, width_cols, channels)
    spread = jnp.zeros((tile_rows, width_cols, channels), jnp.float32)
    kernel_terms = []
    for branch, spacing in enumerate(spacings):
        row_views = {
            row_tap: view_fn(grads_stack[branch], -row_tap * spacing).astype(jnp.float32)
            for row_tap in (-1, 0, 1)
        }
        back_map, tap_grad = backward_taps(row_views, current, taps_all[branch], spacing)
        spread = spread + back_map
        kernel_terms.append(tap_grad)
    kernel_term = jnp.stack(kernel_terms)
    input_grad = (total_grad + plain_back + spread.reshape(pixels, channels)).astype(jnp.bfloat16)
    return (
        input_grad.reshape(tile_rows, width_cols, channels),
        (kernel_term, jnp.stack(point_terms), proj_term),
    )


def general_program(feats, labels, class_weight, depth_kernel, point_weight, proj_weight, head_weight):
    micro_count, tile_rows, width_cols, channels = feats.shape
    space_count = lax.axis_size("space")
    section_count = lax.axis_size("section")
    section_place = lax.axis_index("section")
    factor = loss_scale / (
        micro_count * lax.axis_size("rep") * tile_rows * space_count * width_cols
    )
    weight_table = class_weight.astype(jnp.float32)
    share = channels // space_count
    channel_start = lax.axis_index("space") * share
    taps_all = depth_kernel[0].astype(jnp.float32)
    flat_taps = jnp.tile(
        lax.dynamic_slice_in_dim(taps_all, channel_start, share, 2), (1, 1, width_cols)
    )
    weights = (taps_all, flat_taps, point_weight[0], proj_weight[0], head_weight[0])

    def shift_space(source, devices_by):
        return passed_along(source, "space", devices_by)

    tools = (make_view(shift_space, space_count), None, None, None, None, share, channel_start)
    tick_total = micro_count + section_count - 1
    pixels = tile_rows * width_cols
    saved = None
    head_grad = jnp.zeros((channels, 3), jnp.float32)
    arriving = jnp.zeros((tile_rows, width_cols, channels), jnp.bfloat16)
    for moment in range(tick_total):
        batch_raw = moment - section_place
        is_valid = (batch_raw >= 0) & (batch_raw < micro_count)
        batch_slot = jnp.clip(batch_raw, 0, micro_count - 1)
        current = jnp.where(section_place == 0, feats[min(moment, micro_count - 1)], arriving)
        result, head_term, record = forward_block(
            current, weights, fetch(labels, batch_slot), tools, factor, weight_table
        )
        head_grad = head_grad + jnp.where(is_valid, head_term, 0.0)
        if saved is None:
            saved = tuple((jnp.zeros((micro_count,) + item.shape, item.dtype) for item in record))
        saved = tuple(
            (store(buffer, batch_slot, is_valid, item) for buffer, item in zip(saved, record))
        )
        if moment < tick_total - 1:
            arriving = passed_along(result, "section", 1)
    kernel_grad = jnp.zeros((3, 9, channels), jnp.float32)
    point_grad = jnp.zeros((4, channels, channels), jnp.float32)
    proj_grad = jnp.zeros((4 * channels, channels), jnp.float32)
    arriving_grad = jnp.zeros((tile_rows, width_cols, channels), jnp.bfloat16)
    for moment in range(tick_total):
        batch_raw = moment - (section_count - 1 - section_place)
        is_valid = (batch_raw >= 0) & (batch_raw < micro_count)
        batch_slot = jnp.clip(batch_raw, 0, micro_count - 1)
        record = tuple((fetch(buffer, batch_slot) for buffer in saved))
        incoming = arriving_grad.reshape(pixels, channels).astype(jnp.float32)
        input_grad, terms = backward_block(record, incoming, weights, tools)
        kernel_grad = kernel_grad + jnp.where(is_valid, terms[0], 0.0)
        point_grad = point_grad + jnp.where(is_valid, terms[1], 0.0)
        proj_grad = proj_grad + jnp.where(is_valid, terms[2], 0.0)
        if moment < tick_total - 1:
            arriving_grad = passed_along(input_grad, "section", -1)
    local_grads = (kernel_grad[None], point_grad[None], proj_grad[None], head_grad[None])
    summed = lax.psum(
        (local_grads[0], local_grads[1], local_grads[2], local_grads[3]), ("space", "rep")
    )
    return (summed[0], summed[1], summed[2], summed[3])


GROUPS = 2
SHARD = 272
EXTRA = 2048
HEAD_ROW = EXTRA + 32
NT = (((1,), (1,)), ((), ()))
TN = (((0,), (0,)), ((), ()))
F32 = jnp.float32
BF16 = jnp.bfloat16


def rows_from(values, offset):
    if offset == 0:
        return values
    blank = jnp.zeros((abs(offset), values.shape[1]), values.dtype)
    if offset > 0:
        return jnp.concatenate([values[offset:], blank], axis=0)
    return jnp.concatenate([blank, values[:offset]], axis=0)


def lagged_sum(first, second, offset):
    length = first.shape[0]
    if offset >= 0:
        product = first[: length - offset] * second[offset:]
    else:
        product = first[-offset:] * second[:offset]
    return jnp.sum(product, axis=0, keepdims=True)


def dot(first, second, dims=(((1,), (0,)), ((), ()))):
    return lax.dot_general(first, second, dims, preferred_element_type=F32)


def block_kernel(
    factor, spaces, sections,
    feats, labels, class_weight, taps, point, proj, head,
    out_point, out_proj, out_extra,
    xbuf, gbuf, xout, gout, lab, us, vs, ms, hs, total, wide, pair_in, half, ring_in, full,
    feat_send, feat_recv, lab_send, lab_recv, x_send, x_recv, g_send, g_recv,
    p_send, p_recv, r_send, r_recv, a_send, a_recv, c_send, c_recv,
):
    space = lax.axis_index("space")
    section = lax.axis_index("section")
    rep = lax.axis_index("rep")
    last = sections - 1
    step = xbuf.shape[2] // 40
    slot_rows = xbuf.shape[2]
    pixels = 2 * slot_rows
    after = {"section": lax.rem(section + 1, sections)}
    before = {"section": lax.rem(section + sections - 1, sections)}
    twin = {"rep": 1 - rep}

    def along(distance):
        return {"space": lax.rem(space + distance, spaces)}

    def remote(source, target, send, recv, device):
        return pltpu.make_async_remote_copy(
            src_ref=source, dst_ref=target, send_sem=send, recv_sem=recv,
            device_id=device, device_id_type=pl.DeviceIdType.MESH,
        )

    barrier = pltpu.get_barrier_semaphore()
    greeted = [after, before, twin] + [along(k) for k in range(1, spaces)]
    for device in greeted:
        pl.semaphore_signal(barrier, inc=1, device_id=device, device_id_type=pl.DeviceIdType.MESH)
    pl.semaphore_wait(barrier, len(greeted))

    def swap_feats(sent):
        peer = {"space": spaces - 1 if sent == 1 else 0}
        return remote(feats.at[:, sent], xbuf.at[:, 1 - sent], feat_send, feat_recv, peer)

    def swap_labels(sent):
        peer = {"space": spaces - 1 if sent == 1 else 0}
        return remote(labels.at[sent], lab.at[1 - sent], lab_send, lab_recv, peer)

    for place, sent in ((0, 1), (spaces - 1, 0)):
        @pl.when(space == place)
        def _(sent=sent):
            @pl.when(section == 0)
            def _():
                swap_feats(sent).start()
                xbuf[:, 1 - sent] = feats[:, 1 - sent]
            swap_labels(sent).start()
            lab[1 - sent] = labels[1 - sent]

    is_end = (space == 0) | (space == spaces - 1)

    @pl.when(jnp.logical_not(is_end))
    def _():
        @pl.when(section == 0)
        def _():
            xbuf[...] = feats[...]
        lab[...] = labels[...]

    @pl.when(section == last)
    def _():
        gbuf[...] = jnp.zeros_like(gbuf)

    total[pl.ds(EXTRA, 128)] = jnp.zeros((128, total.shape[1]), F32)

    for place, sent in ((0, 1), (spaces - 1, 0)):
        @pl.when(space == place)
        def _(sent=sent):
            @pl.when(section == 0)
            def _():
                swap_feats(sent).wait()
            swap_labels(sent).wait()

    coupled = jnp.where(is_end, 1.0, 0.0).astype(F32)
    tap_rows = taps[...].astype(F32)

    def tap(branch, row_tap, col_tap):
        place = 9 * branch + 3 * (row_tap + 1) + col_tap + 1
        return tap_rows[place : place + 1]

    def end_tap(row_tap, col_tap):
        return tap(0, row_tap, col_tap) * coupled

    def x_copy(group):
        return remote(xout.at[group], xbuf.at[group], x_send.at[group], x_recv.at[group], after)

    def g_copy(group):
        return remote(gout.at[group], gbuf.at[group], g_send.at[group], g_recv.at[group], before)

    for group in range(GROUPS):
        @pl.when(section > 0)
        def _(group=group):
            x_copy(group).wait_recv()

        flat = xbuf[group].reshape(pixels, -1)
        wide_in = flat.astype(F32)
        halves = (wide_in[:slot_rows], wide_in[slot_rows:])
        parts = []
        for branch, spacing in enumerate(spacings):
            done = []
            for slot in range(2):
                running = None
                for col_tap in (-1, 0, 1):
                    term = tap(branch, 0, col_tap) * halves[slot]
                    if branch == 0:
                        term = term + end_tap(1 - 2 * slot, col_tap) * halves[1 - slot]
                    term = rows_from(term, col_tap * spacing * step)
                    running = term if running is None else running + term
                done.append(running.astype(BF16))
            mixed = jnp.concatenate(done, axis=0)
            us[group, branch] = mixed
            parts.append(jnp.maximum(dot(mixed, point[branch]), 0.0).astype(BF16))
        parts.append(jnp.maximum(dot(flat, point[3]), 0.0).astype(BF16))
        joined = jnp.concatenate(parts, axis=1)
        vs[group] = joined
        mixed_pre = dot(joined, proj[...])
        ms[group] = mixed_pre
        result = (wide_in + jnp.maximum(mixed_pre, 0.0)).astype(BF16)
        xout[group] = result.reshape(2, slot_rows, -1)

        @pl.when(section < last)
        def _(group=group):
            x_copy(group).start()

        logits = dot(head[...], result, NT)
        rows = [logits[i : i + 1] for i in range(3)]
        label = jnp.concatenate(
            [lab[slot, group : group + 1, :slot_rows] for slot in range(2)], axis=1
        )
        top = jnp.maximum(jnp.maximum(rows[0], rows[1]), rows[2])
        powers = [jnp.exp(row - top) for row in rows]
        below = powers[0] + powers[1] + powers[2]
        hits = [jnp.where(label == i, 1.0, 0.0).astype(F32) for i in range(3)]
        weight = sum(hits[i] * class_weight[i].astype(F32) for i in range(3)) * factor
        deltas = [weight * (powers[i] / below - hits[i]) for i in range(3)]
        delta = jnp.concatenate(deltas + [jnp.zeros((13, pixels), F32)], axis=0).astype(BF16)
        hs[group] = dot(delta, head[...], TN)
        total[pl.ds(HEAD_ROW, 16)] += dot(delta, result)

    for group in range(GROUPS):
        @pl.when(section < last)
        def _(group=group):
            g_copy(group).wait_recv()

        channels = xbuf.shape[3]
        total_grad = hs[group] + gbuf[group].reshape(pixels, channels).astype(F32)
        gate_mixed = jnp.where(ms[group] > 0, total_grad, 0.0).astype(BF16)
        gates = []
        for branch in range(4):
            columns = pl.ds(branch * channels, channels)
            back = dot(gate_mixed, proj[columns], NT)
            gates.append(jnp.where(vs[group, :, columns] > 0, back, 0.0).astype(BF16))
        grads = [dot(gates[branch], point[branch], NT).astype(BF16).astype(F32) for branch in range(3)]
        split = [(grad[:slot_rows], grad[slot_rows:]) for grad in grads]

        @pl.when(section > 0)
        def _(group=group, gates=gates, total_grad=total_grad, split=split):
            plain = dot(gates[3], point[3], NT)
            done = []
            for slot in range(2):
                running = None
                for branch, spacing in enumerate(spacings):
                    for col_tap in (-1, 0, 1):
                        term = tap(branch, 0, col_tap) * split[branch][slot]
                        if branch == 0:
                            term = term + end_tap(2 * slot - 1, col_tap) * split[branch][1 - slot]
                        term = rows_from(term, -col_tap * spacing * step)
                        running = term if running is None else running + term
                done.append(running)
            input_grad = total_grad + plain + jnp.concatenate(done, axis=0)
            gout[group] = input_grad.astype(BF16).reshape(2, slot_rows, channels)
            g_copy(group).start()

        def put(place, value, group=group):
            if group == 0:
                total[place] = value
            else:
                total[place] += value

        flat = xbuf[group].reshape(pixels, channels)
        for branch in range(4):
            columns = pl.ds(branch * channels, channels)
            put(pl.ds(1024 + branch * channels, channels), dot(vs[group, :, columns], gate_mixed, TN))
            source = us[group, branch] if branch < 3 else flat
            put(columns, dot(source, gates[branch], TN))
        wide_in = flat.astype(F32)
        halves = (wide_in[:slot_rows], wide_in[slot_rows:])
        for branch, spacing in enumerate(spacings):
            for col_tap in (-1, 0, 1):
                offset = col_tap * spacing * step
                row = EXTRA + 9 * branch + col_tap + 1
                centre = lagged_sum(split[branch][0], halves[0], offset)
                centre = centre + lagged_sum(split[branch][1], halves[1], offset)
                total[row + 3 : row + 4] += centre
                if branch == 0:
                    for slot in range(2):
                        cross = lagged_sum(split[0][slot], halves[1 - slot], offset) * coupled
                        place = row + 6 * (1 - slot)
                        total[place : place + 1] += cross

    def shard(index):
        return pl.ds(pl.multiple_of(index * SHARD, 16), SHARD)

    quarter = [lax.rem(space + k, spaces) for k in range(spaces)]

    def pair_copy(k):
        return remote(
            wide.at[shard((1 - rep) * spaces + quarter[k])], pair_in.at[shard(quarter[k])],
            p_send.at[k], p_recv.at[k], twin,
        )

    def ring_copy(k):
        return remote(
            half.at[shard(quarter[k])], ring_in.at[k - 1], r_send.at[k - 1], r_recv.at[k - 1], along(k)
        )

    def gather_copy(k):
        mine = shard(rep * spaces + space)
        return remote(full.at[mine], full.at[mine], a_send.at[k - 1], a_recv.at[k - 1], along(k))

    def cross_copy(k):
        there = shard(rep * spaces + quarter[k])
        return remote(full.at[there], full.at[there], c_send.at[k], c_recv.at[k], twin)

    order = [2, 1, 3, 0]
    for k in order:
        place = shard((1 - rep) * spaces + quarter[k])
        wide[place] = total[place].astype(BF16)
        pair_copy(k).start()
    for k in order:
        pair_copy(k).wait_recv()
        mine = total[shard(rep * spaces + quarter[k])] + pair_in[shard(quarter[k])].astype(F32)
        if k:
            half[shard(quarter[k])] = mine.astype(BF16)
            ring_copy(k).start()
    for k in range(1, spaces):
        ring_copy(k).wait_recv()
        mine = mine + ring_in[k - 1].astype(F32)
    full[shard(rep * spaces + space)] = mine.astype(BF16)
    for k in order[:3]:
        gather_copy(k).start()
    cross_copy(0).start()
    for k in (1, 3, 2):
        gather_copy(k).wait_recv()
        cross_copy(spaces - k).start()
    for k in range(spaces):
        cross_copy(k).wait_recv()
    for branch in range(4):
        out_point[branch] = full[pl.ds(256 * branch, 256)].astype(F32)
    out_proj[...] = full[pl.ds(1024, 1024)].astype(F32)
    out_extra[...] = full[pl.ds(EXTRA, 48)].astype(F32)

    for group in range(GROUPS):
        @pl.when(section < last)
        def _(group=group):
            x_copy(group).wait_send()

        @pl.when(section > 0)
        def _(group=group):
            g_copy(group).wait_send()
    for k in range(spaces):
        pair_copy(k).wait_send()
        cross_copy(k).wait_send()
        if k:
            ring_copy(k).wait_send()
            gather_copy(k).wait_send()


def joined_rows_program(
    feats, labels, class_weight, depth_kernel, point_weight, proj_weight, head_weight
):
    snaps, tile_rows, width_cols, channels = feats.shape
    spaces = lax.axis_size("space")
    sections = lax.axis_size("section")
    factor = loss_scale / (snaps * lax.axis_size("rep") * tile_rows * spaces * width_cols)
    step = tile_rows // GROUPS
    slot_rows = width_cols * step
    pixels = snaps * slot_rows
    maps = feats.reshape(snaps, GROUPS, step, width_cols, channels)
    maps = maps.transpose(1, 0, 3, 2, 4).reshape(GROUPS, snaps, slot_rows, channels)
    marks = labels.reshape(snaps, GROUPS, step, width_cols).transpose(0, 1, 3, 2)
    marks = marks.reshape(snaps, GROUPS, slot_rows)
    marks = jnp.pad(marks, ((0, 0), (0, 8 - GROUPS), (0, 128 - slot_rows)))
    taps = depth_kernel.reshape(27, channels)
    head = jnp.pad(head_weight[0].T, ((0, 13), (0, 0)))
    vmem = pl.BlockSpec(memory_space=pltpu.VMEM)
    dma = pltpu.SemaphoreType.DMA
    outs = pl.pallas_call(
        functools.partial(block_kernel, factor, spaces, sections),
        out_shape=(
            jax.ShapeDtypeStruct((4, channels, channels), F32),
            jax.ShapeDtypeStruct((4 * channels, channels), F32),
            jax.ShapeDtypeStruct((48, channels), F32),
        ),
        in_specs=[vmem, vmem, pl.BlockSpec(memory_space=pltpu.SMEM), vmem, vmem, vmem, vmem],
        out_specs=(vmem, vmem, vmem),
        scratch_shapes=[
            pltpu.VMEM((GROUPS, 2, slot_rows, channels), BF16),
            pltpu.VMEM((GROUPS, 2, slot_rows, channels), BF16),
            pltpu.VMEM((GROUPS, 2, slot_rows, channels), BF16),
            pltpu.VMEM((GROUPS, 2, slot_rows, channels), BF16),
            pltpu.VMEM((2, 8, 128), jnp.int32),
            pltpu.VMEM((GROUPS, 3, pixels, channels), BF16),
            pltpu.VMEM((GROUPS, pixels, 4 * channels), BF16),
            pltpu.VMEM((GROUPS, pixels, channels), F32),
            pltpu.VMEM((GROUPS, pixels, channels), F32),
            pltpu.VMEM((8 * SHARD, channels), F32),
            pltpu.VMEM((8 * SHARD, channels), BF16),
            pltpu.VMEM((4 * SHARD, channels), BF16),
            pltpu.VMEM((4 * SHARD, channels), BF16),
            pltpu.VMEM((3, SHARD, channels), BF16),
            pltpu.VMEM((8 * SHARD, channels), BF16),
            dma, dma, dma, dma,
            dma((GROUPS,)), dma((GROUPS,)), dma((GROUPS,)), dma((GROUPS,)),
            dma((spaces,)), dma((spaces,)),
            dma((spaces - 1,)), dma((spaces - 1,)),
            dma((spaces - 1,)), dma((spaces - 1,)),
            dma((spaces,)), dma((spaces,)),
        ],
        compiler_params=pltpu.CompilerParams(
            collective_id=0, has_side_effects=True, vmem_limit_bytes=40 * 2**20
        ),
        cost_estimate=pl.CostEstimate(
            flops=2 * 2**30, bytes_accessed=8 * 2**20, transcendentals=4096
        ),
        name="pyramid_blocks",
    )(maps, marks, class_weight, taps, point_weight[0], proj_weight[0], head)
    point_grad, proj_grad, extra = outs
    kernel_grad = extra[:27].reshape(1, 3, 9, channels)
    head_grad = extra[32:35].T[None]
    return kernel_grad, point_grad[None], proj_grad[None], head_grad


def rows_pair_up(feats):
    snaps, tile_rows, width_cols, channels = feats.shape
    spaces = lax.axis_size("space")
    return (
        snaps == 2
        and (spaces, lax.axis_size("section"), lax.axis_size("rep")) == (4, 4, 2)
        and spacings[0] == tile_rows * (spaces - 1)
        and spacings[1] >= tile_rows * spaces
        and (tile_rows, width_cols, channels) == (4, 40, 256)
    )


def per_device(feats, *others):
    if rows_pair_up(feats):
        return joined_rows_program(feats, *others)
    return general_program(feats, *others)


def solution(mesh):
    placed = (
        P("rep", "space", None, None),
        P("rep", "space", None),
        P(),
        P("section", None, None, None),
        P("section", None, None, None),
        P("section", None, None),
        P("section", None, None),
    )
    return jax.shard_map(
        per_device,
        mesh=mesh,
        in_specs=placed,
        out_specs=(
            P("section", None, None, None),
            P("section", None, None, None),
            P("section", None, None),
            P("section", None, None),
        ),
        check_vma=False,
    )
```

```python
import functools

import jax
import jax.numpy as jnp
from jax import lax
from jax.experimental import pallas as pl
from jax.experimental.pallas import tpu as pltpu
from jax.sharding import PartitionSpec as P

spacings = (12, 24, 36)
loss_scale = 256.0


def passed_along(block, axis, distance):
    devices = range(lax.axis_size(axis))
    route = [(i - distance, i) for i in devices if i - distance in devices]
    return lax.ppermute(block, axis, route)


def moved(source, offset, axis_dim):
    length = source.shape[axis_dim]
    widths = [(0, 0)] * source.ndim
    widths[axis_dim] = (max(-offset, 0), max(offset, 0))
    padded = jnp.pad(source, widths)
    begin_at = max(offset, 0)
    return lax.slice_in_dim(padded, begin_at, begin_at + length, axis=axis_dim)


def make_view(shift_rows, device_count):

    def piece_from(source, devices_ahead):
        if devices_ahead >= device_count or -devices_ahead >= device_count:
            return jnp.zeros_like(source)
        return shift_rows(source, -devices_ahead)

    def view(source, offset):
        if offset == 0:
            return source
        tile_rows = source.shape[0]
        whole_part = offset // tile_rows
        return piece_from(source, whole_part)

    return view


def forward_taps(row_views, tap_weights, col_step):
    running = jnp.zeros(row_views[0].shape, jnp.float32)
    for row_tap in (-1, 0, 1):
        for col_tap in (-1, 0, 1):
            running = running + tap_weights[3 * (row_tap + 1) + col_tap + 1] * moved(
                row_views[row_tap], col_tap * col_step, 1
            )
    return running


def backward_taps(row_views, base_map, tap_weights, col_step):
    base_wide = base_map.astype(jnp.float32)
    running = jnp.zeros(base_map.shape, jnp.float32)
    kernel_rows = []
    for row_tap in (-1, 0, 1):
        for col_tap in (-1, 0, 1):
            shifted = moved(row_views[row_tap], -col_tap * col_step, 1)
            running = running + tap_weights[3 * (row_tap + 1) + col_tap + 1] * shifted
            partial_sum = jnp.sum(shifted * base_wide, axis=0)
            kernel_rows.append(jnp.sum(partial_sum, axis=0))
    return (running, jnp.stack(kernel_rows))


def matmul(first_op, second_op):
    return jnp.dot(first_op, second_op, preferred_element_type=jnp.float32)


def matmul_trans(first_op, second_op):
    return lax.dot_general(
        first_op, second_op, (((1,), (1,)), ((), ())), preferred_element_type=jnp.float32
    )


def outer(first_op, second_op):
    return lax.dot_general(
        first_op, second_op, (((0,), (0,)), ((), ())), preferred_element_type=jnp.float32
    )


def store(buffer, batch_slot, is_valid, new_value):
    old_value = lax.dynamic_index_in_dim(buffer, batch_slot, 0, keepdims=False)
    return lax.dynamic_update_index_in_dim(
        buffer, jnp.where(is_valid, new_value, old_value), batch_slot, 0
    )


def fetch(buffer, batch_slot):
    return lax.dynamic_index_in_dim(buffer, batch_slot, 0, keepdims=False)


def forward_block(current, weights, label_tile, tools, factor, weight_table):
    taps_all, flat_taps, point_mats, proj_mat, head_mat = weights
    view_fn, to_maps, from_maps = (tools[0], tools[1], tools[2])
    tile_rows, width_cols, channels = current.shape
    pixels = tile_rows * width_cols
    branch_list = []
    for branch, spacing in enumerate(spacings):
        row_views = {
            row_tap: view_fn(current, row_tap * spacing).astype(jnp.float32)
            for row_tap in (-1, 0, 1)
        }
        branch_list.append(forward_taps(row_views, taps_all[branch], spacing).astype(jnp.bfloat16))
    branch_out = jnp.stack(branch_list).reshape(3, pixels, channels)
    extra = ()
    flat_in = current.reshape(pixels, channels)
    pre_acts = [matmul(branch_out[branch], point_mats[branch]) for branch in range(3)]
    pre_acts.append(matmul(flat_in, point_mats[3]))
    joined = jnp.concatenate(
        [jnp.maximum(pre_act, 0.0).astype(jnp.bfloat16) for pre_act in pre_acts], axis=1
    )
    mixed_pre = matmul(joined, proj_mat)
    result = (flat_in.astype(jnp.float32) + jnp.maximum(mixed_pre, 0.0)).astype(jnp.bfloat16)
    logits = matmul(result, head_mat)
    class_ids = jnp.arange(3, dtype=jnp.int32)
    label_flat = label_tile.reshape(pixels, 1)
    onehot = (label_flat == class_ids[None, :]).astype(jnp.float32)
    pixel_weight = jnp.sum(onehot * weight_table[None, :], axis=1)
    chances = jax.nn.softmax(logits, axis=1)
    head_delta = ((factor * pixel_weight)[:, None] * (chances - onehot)).astype(jnp.bfloat16)
    head_term = outer(result, head_delta)
    from_head = matmul_trans(head_delta, head_mat)
    record = (current, branch_out, joined, mixed_pre, from_head) + extra
    return (result.reshape(tile_rows, width_cols, channels), head_term, record)


def backward_block(record, incoming, weights, tools):
    taps_all, flat_taps, point_mats, proj_mat, head_mat = weights
    view_fn, grads_to, grads_from = (tools[0], tools[3], tools[4])
    current, branch_out, joined, mixed_pre, from_head = (
        record[0],
        record[1],
        record[2],
        record[3],
        record[4],
    )
    tile_rows, width_cols, channels = current.shape
    pixels = tile_rows * width_cols
    total_grad = from_head + incoming
    gate_mixed = jnp.where(mixed_pre > 0, total_grad, 0.0).astype(jnp.bfloat16)
    proj_term = outer(joined, gate_mixed)
    back_joined = matmul_trans(gate_mixed, proj_mat)
    gate_joined = jnp.where(joined > 0, back_joined, 0.0).astype(jnp.bfloat16)
    flat_in = current.reshape(pixels, channels)
    point_terms = []
    branch_grads = []
    for branch in range(3):
        part_grad = gate_joined[:, branch * channels : (branch + 1) * channels]
        point_terms.append(outer(branch_out[branch], part_grad))
        branch_grads.append(matmul_trans(part_grad, point_mats[branch]).astype(jnp.bfloat16))
    part_grad = gate_joined[:, 3 * channels :]
    point_terms.append(outer(flat_in, part_grad))
    plain_back = matmul_trans(part_grad, point_mats[3])
    grads_stack = jnp.stack(branch_grads).reshape(3, tile_rows, width_cols, channels)
    spread = jnp.zeros((tile_rows, width_cols, channels), jnp.float32)
    kernel_terms = []
    for branch, spacing in enumerate(spacings):
        row_views = {
            row_tap: view_fn(grads_stack[branch], -row_tap * spacing).astype(jnp.float32)
            for row_tap in (-1, 0, 1)
        }
        back_map, tap_grad = backward_taps(row_views, current, taps_all[branch], spacing)
        spread = spread + back_map
        kernel_terms.append(tap_grad)
    kernel_term = jnp.stack(kernel_terms)
    input_grad = (total_grad + plain_back + spread.reshape(pixels, channels)).astype(jnp.bfloat16)
    return (
        input_grad.reshape(tile_rows, width_cols, channels),
        (kernel_term, jnp.stack(point_terms), proj_term),
    )


def general_program(feats, labels, class_weight, depth_kernel, point_weight, proj_weight, head_weight):
    micro_count, tile_rows, width_cols, channels = feats.shape
    space_count = lax.axis_size("space")
    section_count = lax.axis_size("section")
    section_place = lax.axis_index("section")
    factor = loss_scale / (
        micro_count * lax.axis_size("rep") * tile_rows * space_count * width_cols
    )
    weight_table = class_weight.astype(jnp.float32)
    share = channels // space_count
    channel_start = lax.axis_index("space") * share
    taps_all = depth_kernel[0].astype(jnp.float32)
    flat_taps = jnp.tile(
        lax.dynamic_slice_in_dim(taps_all, channel_start, share, 2), (1, 1, width_cols)
    )
    weights = (taps_all, flat_taps, point_weight[0], proj_weight[0], head_weight[0])

    def shift_space(source, devices_by):
        return passed_along(source, "space", devices_by)

    tools = (make_view(shift_space, space_count), None, None, None, None, share, channel_start)
    tick_total = micro_count + section_count - 1
    pixels = tile_rows * width_cols
    saved = None
    head_grad = jnp.zeros((channels, 3), jnp.float32)
    arriving = jnp.zeros((tile_rows, width_cols, channels), jnp.bfloat16)
    for moment in range(tick_total):
        batch_raw = moment - section_place
        is_valid = (batch_raw >= 0) & (batch_raw < micro_count)
        batch_slot = jnp.clip(batch_raw, 0, micro_count - 1)
        current = jnp.where(section_place == 0, feats[min(moment, micro_count - 1)], arriving)
        result, head_term, record = forward_block(
            current, weights, fetch(labels, batch_slot), tools, factor, weight_table
        )
        head_grad = head_grad + jnp.where(is_valid, head_term, 0.0)
        if saved is None:
            saved = tuple((jnp.zeros((micro_count,) + item.shape, item.dtype) for item in record))
        saved = tuple(
            (store(buffer, batch_slot, is_valid, item) for buffer, item in zip(saved, record))
        )
        if moment < tick_total - 1:
            arriving = passed_along(result, "section", 1)
    kernel_grad = jnp.zeros((3, 9, channels), jnp.float32)
    point_grad = jnp.zeros((4, channels, channels), jnp.float32)
    proj_grad = jnp.zeros((4 * channels, channels), jnp.float32)
    arriving_grad = jnp.zeros((tile_rows, width_cols, channels), jnp.bfloat16)
    for moment in range(tick_total):
        batch_raw = moment - (section_count - 1 - section_place)
        is_valid = (batch_raw >= 0) & (batch_raw < micro_count)
        batch_slot = jnp.clip(batch_raw, 0, micro_count - 1)
        record = tuple((fetch(buffer, batch_slot) for buffer in saved))
        incoming = arriving_grad.reshape(pixels, channels).astype(jnp.float32)
        input_grad, terms = backward_block(record, incoming, weights, tools)
        kernel_grad = kernel_grad + jnp.where(is_valid, terms[0], 0.0)
        point_grad = point_grad + jnp.where(is_valid, terms[1], 0.0)
        proj_grad = proj_grad + jnp.where(is_valid, terms[2], 0.0)
        if moment < tick_total - 1:
            arriving_grad = passed_along(input_grad, "section", -1)
    local_grads = (kernel_grad[None], point_grad[None], proj_grad[None], head_grad[None])
    summed = lax.psum(
        (local_grads[0], local_grads[1], local_grads[2], local_grads[3]), ("space", "rep")
    )
    return (summed[0], summed[1], summed[2], summed[3])


GROUPS = 2
SHARD = 272
PIECES = ((0, 144), (144, 128))
EXTRA = 2048
HEAD_ROW = EXTRA + 32
NT = (((1,), (1,)), ((), ()))
TN = (((0,), (0,)), ((), ()))
F32 = jnp.float32
BF16 = jnp.bfloat16


def rows_from(values, offset):
    if offset == 0:
        return values
    blank = jnp.zeros((abs(offset), values.shape[1]), values.dtype)
    if offset > 0:
        return jnp.concatenate([values[offset:], blank], axis=0)
    return jnp.concatenate([blank, values[:offset]], axis=0)


def lagged_sum(first, second, offset):
    length = first.shape[0]
    if offset >= 0:
        product = first[: length - offset] * second[offset:]
    else:
        product = first[-offset:] * second[:offset]
    return jnp.sum(product, axis=0, keepdims=True)


def dot(first, second, dims=(((1,), (0,)), ((), ()))):
    return lax.dot_general(first, second, dims, preferred_element_type=F32)


def unit_rows(rows, columns):
    down = lax.broadcasted_iota(jnp.int32, (rows, columns), 0)
    across = lax.broadcasted_iota(jnp.int32, (rows, columns), 1)
    return jnp.where(down == across, 1.0, 0.0).astype(BF16)


def widen_kernel(summed, kernel_grad, point_grad, proj_grad, head_grad):
    for branch in range(4):
        point_grad[branch] = summed[pl.ds(256 * branch, 256)].astype(F32)
    proj_grad[...] = summed[pl.ds(1024, 1024)].astype(F32)
    rows = summed[pl.ds(EXTRA, 32)].astype(F32)
    for branch in range(3):
        kernel_grad[branch] = rows[9 * branch : 9 * branch + 9]
    head_grad[...] = dot(summed[pl.ds(HEAD_ROW, 16)], unit_rows(16, 3), TN)


def block_kernel(
    factor, spaces, sections,
    feats, labels, class_weight, small_in, point_in, proj_in,
    full,
    small, point, proj, raw, xbuf, gbuf, xout, gout, lab, us, vs, ms, hs, total, wide, pair_in, half, ring_in,
    load_sems, feat_send, feat_recv, lab_send, lab_recv, x_send, x_recv, g_send, g_recv,
    p_send, p_recv, r_send, r_recv, a_send, a_recv, c_send, c_recv,
):
    space = lax.axis_index("space")
    section = lax.axis_index("section")
    rep = lax.axis_index("rep")
    last = sections - 1
    step = xbuf.shape[2] // 40
    slot_rows = xbuf.shape[2]
    pixels = 2 * slot_rows
    after = {"section": lax.rem(section + 1, sections)}
    before = {"section": lax.rem(section + sections - 1, sections)}
    twin = {"rep": 1 - rep}

    def along(distance):
        return {"space": lax.rem(space + distance, spaces)}

    def remote(source, target, send, recv, device):
        return pltpu.make_async_remote_copy(
            src_ref=source, dst_ref=target, send_sem=send, recv_sem=recv,
            device_id=device, device_id_type=pl.DeviceIdType.MESH,
        )

    loads = [
        pltpu.make_async_copy(source, target, load_sems.at[i])
        for i, (source, target) in enumerate(
            ((small_in, small), (point_in, point), (proj_in, proj))
        )
    ]
    for load in loads:
        load.start()

    barrier = pltpu.get_barrier_semaphore()
    greeted = [after, before, twin] + [along(k) for k in range(1, spaces)]
    for device in greeted:
        pl.semaphore_signal(barrier, inc=1, device_id=device, device_id_type=pl.DeviceIdType.MESH)
    pl.semaphore_wait(barrier, len(greeted))

    def swap_feats(sent, group):
        peer = {"space": spaces - 1 if sent == 1 else 0}
        rows = pl.ds(2 * group, 2)
        return remote(
            feats.at[sent, rows], raw.at[1 - sent, rows], feat_send.at[group], feat_recv.at[group], peer
        )

    def swap_labels(sent):
        peer = {"space": spaces - 1 if sent == 1 else 0}
        return remote(labels.at[sent], lab.at[1 - sent], lab_send, lab_recv, peer)

    def keep(source, target, index, slot):
        return pltpu.make_async_copy(source.at[slot], target.at[slot], load_sems.at[4 + 2 * index + slot])

    ends = ((0, 1), (spaces - 1, 0))
    for place, sent in ends:
        @pl.when(space == place)
        def _(sent=sent):
            @pl.when(section == 0)
            def _():
                for group in range(GROUPS):
                    swap_feats(sent, group).start()
                keep(feats, raw, 0, 1 - sent).start()
            swap_labels(sent).start()
            keep(labels, lab, 1, 1 - sent).start()

    is_end = (space == 0) | (space == spaces - 1)

    @pl.when(jnp.logical_not(is_end))
    def _():
        for slot in range(2):
            @pl.when(section == 0)
            def _(slot=slot):
                keep(feats, raw, 0, slot).start()
            keep(labels, lab, 1, slot).start()

    @pl.when(section == last)
    def _():
        gbuf[...] = jnp.zeros_like(gbuf)

    total[pl.ds(EXTRA, 128)] = jnp.zeros((128, total.shape[1]), F32)

    for place, sent in ends:
        @pl.when(space == place)
        def _(sent=sent):
            @pl.when(section == 0)
            def _():
                keep(feats, raw, 0, 1 - sent).wait()
            keep(labels, lab, 1, 1 - sent).wait()
            swap_labels(sent).wait()

    @pl.when(jnp.logical_not(is_end))
    def _():
        for slot in range(2):
            @pl.when(section == 0)
            def _(slot=slot):
                keep(feats, raw, 0, slot).wait()
            keep(labels, lab, 1, slot).wait()

    for load in loads:
        load.wait()

    coupled = jnp.where(is_end, 1.0, 0.0).astype(F32)
    tap_rows = small[pl.ds(0, 32)].astype(F32)
    head_rows = small[pl.ds(32, 16)]

    def tap(branch, row_tap, col_tap):
        place = 9 * branch + 3 * (row_tap + 1) + col_tap + 1
        return tap_rows[place : place + 1]

    place = lax.broadcasted_iota(jnp.int32, (slot_rows, slot_rows), 0)
    origin = lax.broadcasted_iota(jnp.int32, (slot_rows, slot_rows), 1)
    permute = jnp.where(origin == (place & 1) * 40 + (place >> 1), 1.0, 0.0).astype(BF16)

    column = lax.broadcasted_iota(jnp.int32, (40, slot_rows), 0)
    target = lax.broadcasted_iota(jnp.int32, (40, slot_rows), 1)
    doubled = jnp.where((target >> 1) == column, 1.0, 0.0).astype(BF16)
    odd = (lax.broadcasted_iota(jnp.int32, (1, slot_rows), 1) & 1) == 1
    marks = [dot(lab[slot].astype(F32).astype(BF16), doubled) for slot in range(2)]

    def end_tap(row_tap, col_tap):
        return tap(0, row_tap, col_tap) * coupled

    def x_copy(group):
        return remote(xout.at[group], xbuf.at[group], x_send.at[group], x_recv.at[group], after)

    def g_copy(group):
        return remote(gout.at[group], gbuf.at[group], g_send.at[group], g_recv.at[group], before)

    for group in range(GROUPS):
        @pl.when(section > 0)
        def _(group=group):
            x_copy(group).wait_recv()

        for place, sent in ends:
            @pl.when((section == 0) & (space == place))
            def _(sent=sent, group=group):
                swap_feats(sent, group).wait()

        @pl.when(section == 0)
        def _(group=group):
            for slot in range(2):
                rows = raw[slot, 2 * group : 2 * group + 2].astype(F32)
                rows = rows.reshape(slot_rows, -1).astype(BF16)
                xbuf[group, slot] = dot(permute, rows).astype(BF16)

        flat = xbuf[group].reshape(pixels, -1)
        wide_in = flat.astype(F32)
        halves = (wide_in[:slot_rows], wide_in[slot_rows:])
        parts = []
        for branch, spacing in enumerate(spacings):
            done = []
            for slot in range(2):
                running = None
                for col_tap in (-1, 0, 1):
                    term = tap(branch, 0, col_tap) * halves[slot]
                    if branch == 0:
                        term = term + end_tap(1 - 2 * slot, col_tap) * halves[1 - slot]
                    term = rows_from(term, col_tap * spacing * step)
                    running = term if running is None else running + term
                done.append(running.astype(BF16))
            mixed = jnp.concatenate(done, axis=0)
            us[group, branch] = mixed
            parts.append(jnp.maximum(dot(mixed, point[branch]), 0.0).astype(BF16))
        parts.append(jnp.maximum(dot(flat, point[3]), 0.0).astype(BF16))
        joined = jnp.concatenate(parts, axis=1)
        vs[group] = joined
        mixed_pre = dot(joined, proj[...])
        ms[group] = mixed_pre
        result = (wide_in + jnp.maximum(mixed_pre, 0.0)).astype(BF16)
        xout[group] = result.reshape(2, slot_rows, -1)

        @pl.when(section < last)
        def _(group=group):
            x_copy(group).start()

        logits = dot(head_rows, result, NT)
        rows = [logits[i : i + 1] for i in range(3)]
        label = jnp.concatenate(
            [
                jnp.where(odd, mark[2 * group + 1 : 2 * group + 2], mark[2 * group : 2 * group + 1])
                for mark in marks
            ],
            axis=1,
        )
        top = jnp.maximum(jnp.maximum(rows[0], rows[1]), rows[2])
        powers = [jnp.exp(row - top) for row in rows]
        below = powers[0] + powers[1] + powers[2]
        hits = [jnp.where(label == float(i), 1.0, 0.0).astype(F32) for i in range(3)]
        weight = sum(hits[i] * class_weight[i].astype(F32) for i in range(3)) * factor
        deltas = [weight * (powers[i] / below - hits[i]) for i in range(3)]
        delta = jnp.concatenate(deltas + [jnp.zeros((13, pixels), F32)], axis=0).astype(BF16)
        hs[group] = dot(delta, head_rows, TN)
        total[pl.ds(HEAD_ROW, 16)] += dot(delta, result)

    for group in range(GROUPS):
        @pl.when(section < last)
        def _(group=group):
            g_copy(group).wait_recv()

        channels = xbuf.shape[3]
        total_grad = hs[group] + gbuf[group].reshape(pixels, channels).astype(F32)
        gate_mixed = jnp.where(ms[group] > 0, total_grad, 0.0).astype(BF16)
        gates = []
        for branch in range(4):
            columns = pl.ds(branch * channels, channels)
            back = dot(gate_mixed, proj[columns], NT)
            gates.append(jnp.where(vs[group, :, columns] > 0, back, 0.0).astype(BF16))
        grads = [dot(gates[branch], point[branch], NT).astype(BF16).astype(F32) for branch in range(3)]
        split = [(grad[:slot_rows], grad[slot_rows:]) for grad in grads]

        @pl.when(section > 0)
        def _(group=group, gates=gates, total_grad=total_grad, split=split):
            plain = dot(gates[3], point[3], NT)
            done = []
            for slot in range(2):
                running = None
                for branch, spacing in enumerate(spacings):
                    for col_tap in (-1, 0, 1):
                        term = tap(branch, 0, col_tap) * split[branch][slot]
                        if branch == 0:
                            term = term + end_tap(2 * slot - 1, col_tap) * split[branch][1 - slot]
                        term = rows_from(term, -col_tap * spacing * step)
                        running = term if running is None else running + term
                done.append(running)
            input_grad = total_grad + plain + jnp.concatenate(done, axis=0)
            gout[group] = input_grad.astype(BF16).reshape(2, slot_rows, channels)
            g_copy(group).start()

        def put(place, value, group=group):
            if group == 0:
                total[place] = value
            else:
                total[place] += value

        flat = xbuf[group].reshape(pixels, channels)
        for branch in range(4):
            columns = pl.ds(branch * channels, channels)
            put(pl.ds(1024 + branch * channels, channels), dot(vs[group, :, columns], gate_mixed, TN))
            source = us[group, branch] if branch < 3 else flat
            put(columns, dot(source, gates[branch], TN))
        wide_in = flat.astype(F32)
        halves = (wide_in[:slot_rows], wide_in[slot_rows:])
        for branch, spacing in enumerate(spacings):
            for col_tap in (-1, 0, 1):
                offset = col_tap * spacing * step
                row = EXTRA + 9 * branch + col_tap + 1
                centre = lagged_sum(split[branch][0], halves[0], offset)
                centre = centre + lagged_sum(split[branch][1], halves[1], offset)
                total[row + 3 : row + 4] += centre
                if branch == 0:
                    for slot in range(2):
                        cross = lagged_sum(split[0][slot], halves[1 - slot], offset) * coupled
                        place = row + 6 * (1 - slot)
                        total[place : place + 1] += cross

    def shard(index, piece):
        start, length = PIECES[piece]
        return pl.ds(pl.multiple_of(index * SHARD + start, 16), length)

    quarter = [lax.rem(space + k, spaces) for k in range(spaces)]

    def pair_copy(k, piece):
        return remote(
            wide.at[shard((1 - rep) * spaces + quarter[k], piece)],
            pair_in.at[shard(quarter[k], piece)],
            p_send.at[piece, k], p_recv.at[piece, k], twin,
        )

    def ring_copy(k, piece):
        return remote(
            half.at[shard(quarter[k], piece)], ring_in.at[k - 1, pl.ds(*PIECES[piece])],
            r_send.at[piece, k - 1], r_recv.at[piece, k - 1], along(k),
        )

    def gather_copy(k, piece):
        mine = shard(rep * spaces + space, piece)
        return remote(
            full.at[mine], full.at[mine], a_send.at[piece, k - 1], a_recv.at[piece, k - 1], along(k)
        )

    def cross_copy(k, piece):
        there = shard(rep * spaces + quarter[k], piece)
        return remote(
            full.at[there], full.at[there], c_send.at[piece, k], c_recv.at[piece, k], twin
        )

    order = [2, 1, 3, 0]
    both = range(len(PIECES))
    for piece in both:
        for k in order:
            place = shard((1 - rep) * spaces + quarter[k], piece)
            wide[place] = total[place].astype(BF16)
            pair_copy(k, piece).start()
    kept = []
    for piece in both:
        for k in order:
            pair_copy(k, piece).wait_recv()
            place = shard(quarter[k], piece)
            mine = total[shard(rep * spaces + quarter[k], piece)] + pair_in[place].astype(F32)
            if k:
                half[place] = mine.astype(BF16)
                ring_copy(k, piece).start()
        kept.append(mine)
    for piece in both:
        mine = kept[piece]
        for k in range(1, spaces):
            ring_copy(k, piece).wait_recv()
            mine = mine + ring_in[k - 1, pl.ds(*PIECES[piece])].astype(F32)
        full[shard(rep * spaces + space, piece)] = mine.astype(BF16)
        for k in order[:3]:
            gather_copy(k, piece).start()
        cross_copy(0, piece).start()
    for piece in both:
        for k in (1, 3, 2):
            gather_copy(k, piece).wait_recv()
            cross_copy(spaces - k, piece).start()
    for piece in both:
        for k in range(spaces):
            cross_copy(k, piece).wait_recv()

    for group in range(GROUPS):
        @pl.when(section < last)
        def _(group=group):
            x_copy(group).wait_send()

        @pl.when(section > 0)
        def _(group=group):
            g_copy(group).wait_send()
    for piece in both:
        for k in range(spaces):
            pair_copy(k, piece).wait_send()
            cross_copy(k, piece).wait_send()
            if k:
                ring_copy(k, piece).wait_send()
                gather_copy(k, piece).wait_send()


def joined_rows_program(
    feats, labels, class_weight, depth_kernel, point_weight, proj_weight, head_weight
):
    snaps, tile_rows, width_cols, channels = feats.shape
    spaces = lax.axis_size("space")
    sections = lax.axis_size("section")
    factor = loss_scale / (snaps * lax.axis_size("rep") * tile_rows * spaces * width_cols)
    step = tile_rows // GROUPS
    slot_rows = width_cols * step
    pixels = snaps * slot_rows
    small = jnp.pad(depth_kernel.reshape(27, channels), ((0, 21), (0, 0)))
    small = small + jnp.pad(head_weight[0].T, ((32, 13), (0, 0)))
    vmem = pl.BlockSpec(memory_space=pltpu.VMEM)
    far = pl.BlockSpec(memory_space=pl.ANY)
    dma = pltpu.SemaphoreType.DMA
    outs = pl.pallas_call(
        functools.partial(block_kernel, factor, spaces, sections),
        out_shape=jax.ShapeDtypeStruct((8 * SHARD, channels), BF16),
        in_specs=[far, far, pl.BlockSpec(memory_space=pltpu.SMEM), far, far, far],
        out_specs=vmem,
        scratch_shapes=[
            pltpu.VMEM((48, channels), BF16),
            pltpu.VMEM(point_weight.shape[1:], BF16),
            pltpu.VMEM(proj_weight.shape[1:], BF16),
            pltpu.VMEM(feats.shape, BF16),
            pltpu.VMEM((GROUPS, 2, slot_rows, channels), BF16),
            pltpu.VMEM((GROUPS, 2, slot_rows, channels), BF16),
            pltpu.VMEM((GROUPS, 2, slot_rows, channels), BF16),
            pltpu.VMEM((GROUPS, 2, slot_rows, channels), BF16),
            pltpu.VMEM(labels.shape, jnp.int32),
            pltpu.VMEM((GROUPS, 3, pixels, channels), BF16),
            pltpu.VMEM((GROUPS, pixels, 4 * channels), BF16),
            pltpu.VMEM((GROUPS, pixels, channels), F32),
            pltpu.VMEM((GROUPS, pixels, channels), F32),
            pltpu.VMEM((8 * SHARD, channels), F32),
            pltpu.VMEM((8 * SHARD, channels), BF16),
            pltpu.VMEM((4 * SHARD, channels), BF16),
            pltpu.VMEM((4 * SHARD, channels), BF16),
            pltpu.VMEM((3, SHARD, channels), BF16),
            dma((8,)), dma((GROUPS,)), dma((GROUPS,)), dma, dma,
            dma((GROUPS,)), dma((GROUPS,)), dma((GROUPS,)), dma((GROUPS,)),
            dma((len(PIECES), spaces)), dma((len(PIECES), spaces)),
            dma((len(PIECES), spaces - 1)), dma((len(PIECES), spaces - 1)),
            dma((len(PIECES), spaces - 1)), dma((len(PIECES), spaces - 1)),
            dma((len(PIECES), spaces)), dma((len(PIECES), spaces)),
        ],
        compiler_params=pltpu.CompilerParams(
            collective_id=0, has_side_effects=True, vmem_limit_bytes=62 * 2**20
        ),
        cost_estimate=pl.CostEstimate(
            flops=2 * 2**30, bytes_accessed=8 * 2**20, transcendentals=4096
        ),
        name="pyramid_blocks",
    )(feats, labels, class_weight, small, point_weight[0], proj_weight[0])
    kernel_grad, point_grad, proj_grad, head_grad = pl.pallas_call(
        widen_kernel,
        out_shape=(
            jax.ShapeDtypeStruct((3, 9, channels), F32),
            jax.ShapeDtypeStruct((4, channels, channels), F32),
            jax.ShapeDtypeStruct((4 * channels, channels), F32),
            jax.ShapeDtypeStruct((channels, 3), F32),
        ),
        in_specs=[vmem],
        out_specs=(vmem, vmem, vmem, vmem),
        compiler_params=pltpu.CompilerParams(vmem_limit_bytes=16 * 2**20),
        name="widen",
    )(outs)
    return kernel_grad[None], point_grad[None], proj_grad[None], head_grad[None]


def rows_pair_up(feats):
    snaps, tile_rows, width_cols, channels = feats.shape
    spaces = lax.axis_size("space")
    return (
        snaps == 2
        and (spaces, lax.axis_size("section"), lax.axis_size("rep")) == (4, 4, 2)
        and spacings[0] == tile_rows * (spaces - 1)
        and spacings[1] >= tile_rows * spaces
        and (tile_rows, width_cols, channels) == (4, 40, 256)
    )


def per_device(feats, *others):
    if rows_pair_up(feats):
        return joined_rows_program(feats, *others)
    return general_program(feats, *others)


def solution(mesh):
    placed = (
        P("rep", "space", None, None),
        P("rep", "space", None),
        P(),
        P("section", None, None, None),
        P("section", None, None, None),
        P("section", None, None),
        P("section", None, None),
    )
    return jax.shard_map(
        per_device,
        mesh=mesh,
        in_specs=placed,
        out_specs=(
            P("section", None, None, None),
            P("section", None, None, None),
            P("section", None, None),
            P("section", None, None),
        ),
        check_vma=False,
    )
```
